128 devices in a mesh: seq: 32 (over z_lo, y, x), head: 4 (over z_hi, core).
Axes of the slice: x: 4, y: 4, z: 4 (z_hi: 2, z_lo: 2; z = z_hi * 2 + z_lo), core: 2. Of those that a mesh axis runs over, the one named last changes fastest.
Arguments:
- row_queries: bfloat16 [32768, 2048], P('seq', 'head'), may hold values from -200 to 200
- row_keys: bfloat16 [32768, 2048], P('seq', 'head'), may hold values from -6 to 6
- row_values: bfloat16 [32768, 2048], P('seq', 'head'), may hold values from -6 to 6
- residual_in: bfloat16 [32768, 4096], P(('seq', 'head')), may hold values from -6 to 6
- out_weight: bfloat16 [2048, 4096], P('head', 'seq'), may hold values from -0.25 to 0.25
- norm_gain: float32 [4096], replicated, may hold values from 0.1 to 1.9
- qkv_weight: bfloat16 [4096, 16, 3, 128], P('seq', 'head'), may hold values from -4 to 4
Outputs:
- residual_out: bfloat16 [32768, 4096], P(('seq', 'head'))
- column_out: bfloat16 [32768, 2048], P('seq', 'head')
The draws below stay inside these ranges and needn't reach their ends.
All inputs are finite; a program needn't handle non-finite values.
Results may differ from the reference program's by a relative error of at most 0.0091.
Values may be sent and summed in bfloat16 or wider, within the bound.
A program may use at most 128 MiB of HBM per device.

```python
import jax
import jax.numpy as jnp
from jax import lax

D = 4096
HEADS = 16
HD = 128
COLS = 512
TOKENS = 32768


def shared_keys(key):
    return jnp.clip(jax.random.normal(key, (TOKENS, HEADS * HD), jnp.float32), -6.0, 6.0)


def draw_row_keys(key, part):
    return shared_keys(key).astype(jnp.bfloat16)


def draw_row_queries(key, part):
    key = jax.random.fold_in(key, 11)
    first = jax.random.fold_in(key, 0)
    result = jnp.clip(jax.random.normal(first, (TOKENS, HEADS * HD), jnp.float32), -6.0, 6.0) * 2.0
    return result.astype(jnp.bfloat16)


def draw_qkv_weight(key, part):
    key = jax.random.fold_in(key, 5)
    first = jax.random.fold_in(key, 0)
    weights = jnp.clip(jax.random.normal(first, (D, HEADS, 3, HD), jnp.float32), -6.0, 6.0) * D ** (-0.5)
    return weights.astype(jnp.bfloat16)


def levels(stream_key, extent, cuts, low, top_value):
    def one(position, blocks):
        draws = jax.random.uniform(jax.random.fold_in(jax.random.fold_in(stream_key, 6), position), (blocks,), jnp.float32, low / len(cuts), top_value / len(cuts))
        return jnp.repeat(jnp.exp(draws), extent[position] // blocks).reshape((-1,) + (1,) * (len(extent) - position - 1))

    factor_of = one(*cuts[0])
    for cut in cuts[1:]:
        factor_of = factor_of * one(*cut)
    return factor_of


def normal_values(rng, shape, deviation, bound, shards=(), held_as=jnp.bfloat16):
    array = deviation * jax.random.normal(rng, shape, jnp.float32)
    if shards:
        array = array * levels(rng, shape, shards, -0.22, 0.18)
    return jnp.clip(array, -bound, bound).astype(held_as)


def setup_inputs(seed: int = 0) -> dict:
    key_of = jax.random.split(jax.random.key(seed), 8)
    return {
        "row_queries": draw_row_queries(jax.random.fold_in(key_of[7], 71), 0),
        "row_keys": draw_row_keys(jax.random.fold_in(key_of[7], 71), 0),
        "row_values": normal_values(key_of[2], (TOKENS, HEADS * HD), 1.0, 6.0, ((0, 32), (1, 4))),
        "residual_in": normal_values(key_of[3], (TOKENS, D), 1.0, 6.0, ((0, 128),)),
        "out_weight": normal_values(key_of[4], (HEADS * HD, D), (4 * HD) ** -0.5, 0.25, ((0, 4), (1, 32))),
        "norm_gain": jnp.clip(1.0 + 0.18 * jax.random.normal(key_of[5], (D,), jnp.float32), 0.1, 1.9),
        "qkv_weight": draw_qkv_weight(jax.random.fold_in(key_of[7], 71), 0),
    }


epsilon = 1e-05

def band_attention(queries, keys, values, has_prev):
    width = queries.shape[0]
    scores = jnp.einsum('qhd,khd->hqk', queries.astype(jnp.float32), keys.astype(jnp.float32)) * queries.shape[-1] ** (-0.5)
    query_col = jnp.arange(width, dtype=jnp.int32)[:, None]
    key_col = jnp.arange(2 * width, dtype=jnp.int32)[None, :]
    allowed = jnp.where(key_col < width, (key_col > query_col) & has_prev, key_col - width <= query_col)
    scores = jnp.where(allowed[None], scores, -jnp.inf)
    shifted = jnp.exp(scores - lax.optimization_barrier(jnp.max(scores, -1, keepdims=True)))
    weights = (shifted / lax.optimization_barrier(jnp.sum(shifted, -1, keepdims=True))).astype(jnp.bfloat16)
    return jnp.einsum('hqk,khd->qhd', weights.astype(jnp.float32), values.astype(jnp.float32)).astype(jnp.bfloat16)

def column_head(block):
    queries = block[:, :, 0].astype(jnp.float32)
    keys = block[:, :, 1].astype(jnp.float32)
    values = block[:, :, 2].astype(jnp.float32)
    scores = jnp.einsum('rcd,scd->crs', queries, keys) * queries.shape[-1] ** (-0.5)
    height = block.shape[0]
    allowed = jnp.arange(height, dtype=jnp.int32)[None, :] <= jnp.arange(height, dtype=jnp.int32)[:, None]
    scores = jnp.where(allowed[None], scores, -jnp.inf)
    shifted = jnp.exp(scores - lax.optimization_barrier(jnp.max(scores, -1, keepdims=True)))
    weights = (shifted / lax.optimization_barrier(jnp.sum(shifted, -1, keepdims=True))).astype(jnp.bfloat16)
    return jnp.einsum('crs,scd->rcd', weights.astype(jnp.float32), values).astype(jnp.bfloat16)

def reference(row_queries, row_keys, row_values, residual_in, out_weight, norm_gain, qkv_weight):
    grid_rows = TOKENS // COLS
    shape = (grid_rows, COLS, HEADS, HD)
    queries = row_queries.reshape(shape)
    keys = row_keys.reshape(shape)
    values = row_values.reshape(shape)
    keys_prev = jnp.concatenate([jnp.zeros_like(keys[:1]), keys[:-1]], 0)
    values_prev = jnp.concatenate([jnp.zeros_like(values[:1]), values[:-1]], 0)
    row_index = jnp.arange(grid_rows, dtype=jnp.int32)

    def one_row(item):
        query_row, key_row, value_row, key_back, value_back, number = item
        return band_attention(query_row, jnp.concatenate([key_back, key_row], 0), jnp.concatenate([value_back, value_row], 0), number > 0)
    row_out = lax.map(one_row, (queries, keys, values, keys_prev, values_prev, row_index)).reshape(TOKENS, HEADS * HD)
    projected = jnp.dot(row_out, out_weight, preferred_element_type=jnp.float32)
    residual_out = (residual_in.astype(jnp.float32) + projected).astype(jnp.bfloat16)
    stream = residual_out.astype(jnp.float32)
    center = stream - lax.optimization_barrier(jnp.mean(stream, -1, keepdims=True))
    variance = lax.optimization_barrier(jnp.mean(center * center, -1, keepdims=True))
    normed = (center * lax.rsqrt(variance + epsilon) * norm_gain).astype(jnp.bfloat16)
    column_qkv = jnp.dot(normed, qkv_weight.reshape(D, HEADS * 3 * HD), preferred_element_type=jnp.float32).astype(jnp.bfloat16)
    column_qkv = column_qkv.reshape(grid_rows, COLS, HEADS, 3, HD)
    per_head = lax.map(column_head, jnp.moveaxis(column_qkv, 2, 0))
    column_out = jnp.moveaxis(per_head, 0, 2).reshape(TOKENS, HEADS * HD)
    return (residual_out, column_out)
```

```python
import functools

import jax
import jax.numpy as jnp
from jax import lax
from jax.experimental import pallas as pl
from jax.experimental.pallas import tpu as pltpu
from jax.sharding import PartitionSpec as P

HD = 128
COLS = 512
GROUPS = 4
MESH = pl.DeviceIdType.MESH
EPS = 1e-05
EXP2_SCALE = HD ** (-0.5) * 1.4426950408889634
BF16 = jnp.bfloat16
F32 = jnp.float32


def aligned(value, by):
    return pl.multiple_of(value, by)


def ring4(value):
    return lax.rem(value + 8, 4)


class Place:
    def __init__(self):
        self.s = lax.axis_index("seq")
        self.h = lax.axis_index("head")
        self.z_lo = lax.div(self.s, 16)
        self.yx = lax.rem(self.s, 16)
        self.y = lax.div(self.yx, 4)
        self.x = lax.rem(self.s, 4)
        self.z_hi = lax.div(self.h, 2)
        self.core = lax.rem(self.h, 2)
        self.z = self.z_hi * 2 + self.z_lo

    def device(self, z, y, x, core):
        return (lax.rem(z, 2) * 16 + y * 4 + x, lax.div(z, 2) * 2 + core)

    def first(self, half, d):
        if half == 0:
            return self.device(self.z, self.y, ring4(self.x + d), self.core)
        return self.device(self.z, ring4(self.y + d), self.x, self.core)

    def second(self, half, d):
        return self.first(1 - half, d)

    def block(self, half, df, ds):
        if half == 0:
            return ring4(self.y - ds), ring4(self.x - df)
        return ring4(self.y - df), ring4(self.x - ds)

    def sibling(self):
        return (self.s, self.z_hi * 2 + 1 - self.core)

    def at_z(self, d):
        return self.device(ring4(self.z + d), self.y, self.x, self.core)


def remote(src, dst, send, recv, device):
    return pltpu.make_async_remote_copy(
        src_ref=src, dst_ref=dst, send_sem=send, recv_sem=recv, device_id=device, device_id_type=MESH
    )


def greet(barrier, device):
    pl.semaphore_signal(barrier, inc=1, device_id=device, device_id_type=MESH)


def contract_last(a, b):
    return lax.dot_general(a, b, (((1,), (1,)), ((), ())), preferred_element_type=F32)


def dot(a, b):
    return jnp.dot(a, b, preferred_element_type=F32)


def band_head(queries, keys_prev, keys, values_prev, values, has_prev):
    n = queries.shape[0]
    row = lax.broadcasted_iota(jnp.int32, (n, n), 0)
    col = lax.broadcasted_iota(jnp.int32, (n, n), 1)
    here = col <= row
    back = contract_last(queries, keys_prev)
    back = jnp.where(has_prev, back, -jnp.inf)
    scores = jnp.where(here, contract_last(queries, keys), back)
    top = jnp.max(scores, -1, keepdims=True)
    weights = jnp.exp2((scores - top) * EXP2_SCALE)
    total = jnp.sum(weights, -1, keepdims=True)
    own = jnp.where(here, weights, 0.0).astype(BF16)
    prev = jnp.where(here, 0.0, weights).astype(BF16)
    result = dot(own, values) + dot(prev, values_prev)
    return (result / total).astype(BF16)


def front(
    q, k, v, res, wo, gain, res_out, normed,
    halo, rows, rows_in, w, part, part_in, acc,
    halo_s, halo_r, row_s, row_r, z_s, z_r, f_s, f_r, s_s, s_r, o_s, o_r, p_s, p_r,
):
    me = Place()
    here = (me.s, me.h)
    features = q.shape[1]
    depth = wo.shape[0]
    half_rows, quarter = depth // 2, depth // 4
    share = res.shape[0]
    chunk = 512
    chunks = res.shape[1] // chunk

    barrier = pltpu.get_barrier_semaphore()
    last = me.s == 31

    @pl.when(me.s > 0)
    def _():
        greet(barrier, (me.s - 1, me.h))

    for d in (1, 2, 3):
        greet(barrier, me.at_z(d))
        greet(barrier, me.first(0, d))
        greet(barrier, me.first(1, d))
    greet(barrier, me.sibling())

    @pl.when(last)
    def _():
        pl.semaphore_wait(barrier, 10)

    @pl.when(jnp.logical_not(last))
    def _():
        pl.semaphore_wait(barrier, 11)

    def halo_copy(which):
        source = (k, v)[which]
        return remote(
            source.at[pl.ds(COLS, COLS)], halo.at[which], halo_s.at[which], halo_r.at[which],
            (lax.rem(me.s + 1, 32), me.h),
        )

    @pl.when(jnp.logical_not(last))
    def _():
        halo_copy(0).start()
        halo_copy(1).start()

    @pl.when(me.s == 0)
    def _():
        halo[...] = jnp.zeros_like(halo)

    def slot(dz, half, df, ds, offset, count):
        zz = ring4(me.z - dz)
        yy, xx = me.block(half, df, ds)
        return w.at[
            pl.ds(aligned(lax.div(zz, 2) * depth + offset, 16), count),
            pl.ds(aligned((lax.rem(zz, 2) * 16 + yy * 4 + xx) * 128, 128), 128),
        ]

    def z_copy(d):
        spot = slot(0, 0, 0, 0, 0, depth)
        return remote(wo, spot, z_s.at[d - 1], z_r.at[d - 1], me.at_z(d))

    def z_land(d):
        spot = slot(d, 0, 0, 0, 0, depth)
        return remote(spot, spot, z_s.at[d - 1], z_r.at[d - 1], me.at_z(d))

    def f_copy(half, dz, d, landing=False):
        spot = slot(dz, half, d if landing else 0, 0, half * half_rows, half_rows)
        return remote(spot, spot, f_s.at[half, dz, d - 1], f_r.at[half, dz, d - 1], me.first(half, d))

    def s_copy(half, way, dz, df, landing=False):
        step = 1 - 2 * way
        spot = slot(dz, half, df, step if landing else 0, half * half_rows, half_rows)
        i = dz * 4 + df
        return remote(spot, spot, s_s.at[half, way, i], s_r.at[half, way, i], me.second(half, step))

    def o_copy(half, way, dz, df, landing=False):
        step = 1 - 2 * way
        spot = slot(dz, half, df, 2 * step if landing else step, half * half_rows + way * quarter, quarter)
        i = dz * 4 + df
        return remote(spot, spot, o_s.at[half, way, i], o_r.at[half, way, i], me.second(half, step))

    for d in (1, 2, 3):
        z_copy(d).start()
    w[
        pl.ds(aligned(me.z_hi * depth, 16), depth), pl.ds(aligned(me.s * 128, 128), 128)
    ] = wo[...]

    def spread(dz):
        for half in (0, 1):
            for d in (1, 3, 2):
                f_copy(half, dz, d).start()
        for half in (0, 1):
            for way in (0, 1):
                s_copy(half, way, dz, 0).start()

    spread(0)

    def attend(line, keys_prev, values_prev, has_prev):
        top = line * COLS
        for g in range(GROUPS):
            cols = slice(g * HD, (g + 1) * HD)
            rows[line, :, cols] = band_head(
                q[top : top + COLS, cols],
                keys_prev[:, cols],
                k[top : top + COLS, cols],
                values_prev[:, cols],
                v[top : top + COLS, cols],
                has_prev,
            )

    def row_copy():
        return remote(rows.at[1 - me.z_hi], rows_in, row_s.at[0], row_r.at[0], me.at_z(2))

    attend(1, k.at[pl.ds(0, COLS)], v.at[pl.ds(0, COLS)], True)

    @pl.when(me.z_hi == 0)
    def _():
        row_copy().start()

    @pl.loop(1, 4)
    def _(dz):
        z_land(dz).wait_recv()
        spread(dz)

    @pl.loop(0, 4)
    def _(dz):
        for df in (1, 3, 2):
            for half in (0, 1):
                f_copy(half, dz, df, True).wait_recv()
                for way in (0, 1):
                    s_copy(half, way, dz, df).start()

    @pl.when(me.s > 0)
    def _():
        halo_copy(0).wait_recv()
        halo_copy(1).wait_recv()

    attend(0, halo.at[0], halo.at[1], me.s > 0)

    @pl.when(me.z_hi == 1)
    def _():
        row_copy().start()

    @pl.loop(0, 4)
    def _(dz):
        for df in range(4):
            for half in (0, 1):
                for way in (0, 1):
                    s_copy(half, way, dz, df, True).wait_recv()
                    o_copy(half, way, dz, df).start()

    @pl.loop(0, 4)
    def _(dz):
        for df in range(4):
            for half in (0, 1):
                for way in (0, 1):
                    o_copy(half, way, dz, df, True).wait_recv()

    row_copy().wait_recv()

    def product(of_core, columns):
        mine = pl.ds(aligned(of_core * share, 16), share)
        kept = dot(rows[me.z_hi, mine, :], w[pl.ds(aligned(me.z_hi * depth, 16), depth), columns])
        came = dot(rows_in[mine, :], w[pl.ds(aligned((1 - me.z_hi) * depth, 16), depth), columns])
        return kept + came

    def p_copy(n):
        columns = pl.ds(aligned(n * chunk, chunk), chunk)
        return remote(part.at[:, columns], part_in.at[:, columns], p_s.at[n], p_r.at[n], me.sibling())

    @pl.loop(0, chunks)
    def _(n):
        columns = pl.ds(aligned(n * chunk, chunk), chunk)
        part[:, columns] = product(1 - me.core, columns)
        p_copy(n).start()
        acc[:, columns] = product(me.core, columns) + res[:, columns].astype(F32)

    def settle(n, total):
        columns = pl.ds(aligned(n * chunk, chunk), chunk)
        p_copy(n).wait_recv()
        value = (acc[:, columns] + part_in[:, columns]).astype(BF16)
        res_out[:, columns] = value
        return total + jnp.sum(value.astype(F32), -1, keepdims=True)

    total = lax.fori_loop(0, chunks, settle, jnp.zeros((share, 1), F32))
    width = res.shape[1]
    mean = total / width

    def spread_of(n, total):
        columns = pl.ds(aligned(n * chunk, chunk), chunk)
        center = res_out[:, columns].astype(F32) - mean
        return total + jnp.sum(center * center, -1, keepdims=True)

    variance = lax.fori_loop(0, chunks, spread_of, jnp.zeros((share, 1), F32)) / width
    scale = lax.rsqrt(variance + EPS)

    @pl.loop(0, chunks)
    def _(n):
        columns = pl.ds(aligned(n * chunk, chunk), chunk)
        center = res_out[:, columns].astype(F32) - mean
        normed[:, columns] = (center * scale * gain[:, columns]).astype(BF16)

    @pl.when(jnp.logical_not(last))
    def _():
        halo_copy(0).wait_send()
        halo_copy(1).wait_send()

    row_copy().wait_send()
    for d in (1, 2, 3):
        z_copy(d).wait_send()

    @pl.loop(0, 4)
    def _(dz):
        for half in (0, 1):
            for d in (1, 2, 3):
                f_copy(half, dz, d).wait_send()
            for way in (0, 1):
                for df in range(4):
                    s_copy(half, way, dz, df).wait_send()
                    o_copy(half, way, dz, df).wait_send()

    @pl.loop(0, chunks)
    def _(n):
        p_copy(n).wait_send()


def back(
    normed, wq, out, n_buf, w, qkv, att, ship,
    e_s, e_r, f_s, f_r, s_s, s_r, o_s, o_r, b_s, b_r,
    n_s, n_r, zn_s, zn_r, zo_s, zo_r, out_s, out_r, own_sem,
):
    me = Place()
    depth = wq.shape[0]
    half_rows, quarter = depth // 2, depth // 4
    width = normed.shape[1]
    stays = me.z_lo == me.core
    line = 16

    barrier = pltpu.get_barrier_semaphore()

    def in_plane(d):
        spot = lax.rem(me.yx + d + 32, 16)
        return me.device(me.z, lax.div(spot, 4), lax.rem(spot, 4), me.core)

    for d in range(1, 16):
        greet(barrier, in_plane(d))
    greet(barrier, me.at_z(1))
    greet(barrier, me.at_z(3))
    greet(barrier, me.sibling())

    swap = (me.core * 16 + me.yx, me.z_hi * 2 + me.z_lo)

    @pl.when(jnp.logical_not(stays))
    def _():
        greet(barrier, swap)

    def source(d):
        spot = lax.rem(me.yx + lax.rem(d, 16), 16)
        core = lax.rem(me.core + lax.div(d, 16), 2)
        return me.device(me.h, lax.div(spot, 4), lax.rem(spot, 4), core)

    @pl.loop(1, 32)
    def _(d):
        greet(barrier, source(d))

    @pl.when(jnp.logical_not(stays))
    def _():
        greet(barrier, source(0))

    @pl.when(stays)
    def _():
        pl.semaphore_wait(barrier, 15 + 3 + 31)

    @pl.when(jnp.logical_not(stays))
    def _():
        pl.semaphore_wait(barrier, 15 + 3 + 1 + 32)

    def slot(core, half, df, ds, offset, count):
        yy, xx = me.block(half, df, ds)
        return w.at[pl.ds(aligned((core * 16 + yy * 4 + xx) * depth + offset, 16), count)]

    def swap_copy():
        return remote(
            wq, w.at[pl.ds(aligned(me.s * depth, 16), depth)], e_s.at[0], e_r.at[0], swap
        )

    def swap_land():
        spot = slot(me.core, 0, 0, 0, 0, depth)
        return remote(spot, spot, e_s.at[0], e_r.at[0], swap)

    @pl.when(jnp.logical_not(stays))
    def _():
        swap_copy().start()

    def n_spot(dz, d):
        rows = pl.ds(aligned(lax.rem(me.yx - d + 32, 16) * line, line), line)
        return n_buf.at[ring4(me.z - dz), rows]

    def n_copy(d, landing=False):
        if landing:
            spot = n_spot(0, d)
            return remote(spot, spot, n_s.at[d], n_r.at[d], in_plane(d))
        src = normed.at[pl.ds(aligned(lax.rem(me.yx + d, 16) * line, line), line)]
        return remote(src, n_spot(0, 0), n_s.at[d], n_r.at[d], in_plane(d))

    def zn_copy(way, d, landing=False):
        step = 1 - 2 * way
        spot = n_spot(step if landing else 0, d)
        return remote(spot, spot, zn_s.at[way, d], zn_r.at[way, d], me.at_z(step))

    def zo_copy(way, d, landing=False):
        step = 1 - 2 * way
        spot = n_spot(2 * step if landing else step, d).at[:, pl.ds(way * (width // 2), width // 2)]
        return remote(spot, spot, zo_s.at[way, d], zo_r.at[way, d], me.at_z(step))

    n_buf[me.z, pl.ds(aligned(me.yx * line, line), line), :] = normed[
        pl.ds(aligned(me.yx * line, line), line), :
    ]
    for way in (0, 1):
        zn_copy(way, 0).start()

    @pl.loop(1, 16)
    def _(d):
        n_copy(d).start()

    @pl.when(stays)
    def _():
        w[pl.ds(aligned(me.s * depth, 16), depth), :] = wq[...]

    @pl.when(jnp.logical_not(stays))
    def _():
        swap_land().wait_recv()

    def f_copy(half, d, landing=False):
        spot = slot(me.core, half, d if landing else 0, 0, half * half_rows, half_rows)
        return remote(spot, spot, f_s.at[half, d - 1], f_r.at[half, d - 1], me.first(half, d))

    def s_copy(half, way, df, landing=False):
        step = 1 - 2 * way
        spot = slot(me.core, half, df, step if landing else 0, half * half_rows, half_rows)
        return remote(spot, spot, s_s.at[half, way, df], s_r.at[half, way, df], me.second(half, step))

    def o_copy(half, way, df, landing=False):
        step = 1 - 2 * way
        spot = slot(me.core, half, df, 2 * step if landing else step, half * half_rows + way * quarter, quarter)
        return remote(spot, spot, o_s.at[half, way, df], o_r.at[half, way, df], me.second(half, step))

    def b_copy(half, df, ds, landing=False):
        core = 1 - me.core if landing else me.core
        spot = slot(core, half, df, ds, half * half_rows, half_rows)
        i = df * 4 + ring4(ds)
        return remote(spot, spot, b_s.at[half, i], b_r.at[half, i], me.sibling())

    for half in (0, 1):
        for d in (1, 3, 2):
            f_copy(half, d).start()
    for half in (0, 1):
        for way in (0, 1):
            s_copy(half, way, 0).start()
        b_copy(half, 0, 0).start()

    @pl.loop(1, 16)
    def _(d):
        n_copy(d, True).wait_recv()
        for way in (0, 1):
            zn_copy(way, d).start()

    for df in (1, 3, 2):
        for half in (0, 1):
            f_copy(half, df, True).wait_recv()
            for way in (0, 1):
                s_copy(half, way, df).start()
            b_copy(half, df, 0).start()
    for df in (0, 1, 3, 2):
        for half in (0, 1):
            for way in (0, 1):
                s_copy(half, way, df, True).wait_recv()
                o_copy(half, way, df).start()
                b_copy(half, df, 1 - 2 * way).start()

    @pl.loop(0, 16)
    def _(d):
        for way in (0, 1):
            zn_copy(way, d, True).wait_recv()
            zo_copy(way, d).start()

    for df in (0, 1, 3, 2):
        for half in (0, 1):
            for way in (0, 1):
                o_copy(half, way, df, True).wait_recv()
            b_copy(half, df, 2).start()

    for half in (0, 1):
        for df in range(4):
            for ds in range(4):
                b_copy(half, df, ds, True).wait_recv()

    size = line * 16
    at = lax.broadcasted_iota(jnp.int32, (size, size), 0)
    to = lax.broadcasted_iota(jnp.int32, (size, size), 1)
    turn = (to == (at & 15) * 16 + (at >> 4)).astype(F32).astype(BF16)
    chunk = 512

    def project(dz):
        zz = ring4(me.z - dz)

        @pl.loop(0, w.shape[1] // chunk)
        def _(n):
            columns = pl.ds(aligned(n * chunk, chunk), chunk)
            value = dot(n_buf[zz], w[:, columns]).astype(BF16)
            turned = dot(turn, value).astype(BF16)
            qkv[:, pl.ds(aligned(zz * 16, 16), 16), columns] = turned.reshape(16, 16, chunk)

    project(0)
    project(1)
    project(3)

    @pl.loop(0, 16)
    def _(d):
        for way in (0, 1):
            zo_copy(way, d, True).wait_recv()

    project(2)

    grid_row = 2 * (((at >> 4) & 1) * 16 + (at & 15)) + ((at >> 5) & 1)
    grid_row_k = 2 * (((to >> 4) & 1) * 16 + (to & 15)) + ((to >> 5) & 1)
    allowed = ((at >> 6) == (to >> 6)) & (grid_row_k <= grid_row)

    @pl.loop(0, 4)
    def _(block):
        columns = pl.ds(block * 4, 4)
        for g in range(GROUPS):
            base = g * 3 * HD
            queries = qkv[columns, :, base : base + HD].reshape(size, HD)
            keys = qkv[columns, :, base + HD : base + 2 * HD].reshape(size, HD)
            values = qkv[columns, :, base + 2 * HD : base + 3 * HD].reshape(size, HD)
            scores = jnp.where(allowed, contract_last(queries, keys), -jnp.inf)
            top = jnp.max(scores, -1, keepdims=True)
            weights = jnp.exp2((scores - top) * EXP2_SCALE)
            total = jnp.sum(weights, -1, keepdims=True)
            result = (dot(weights.astype(BF16), values) / total).astype(BF16)
            att[columns, :, g * HD : (g + 1) * HD] = result.reshape(4, 64, HD)

    for zz in range(4):
        plane = att[:, zz * 16 : (zz + 1) * 16, :].reshape(size, GROUPS * HD)
        ship[zz // 2, zz % 2] = dot(turn, plane).astype(BF16)

    mine = pl.ds(aligned(me.core * 256 + me.yx * line, line), line)

    def out_copy(d):
        spot = lax.rem(me.yx - lax.rem(d, 16) + 16, 16)
        z_lo = lax.rem(me.z_lo + lax.div(d, 16), 2)
        src = ship.at[:, z_lo, pl.ds(aligned(spot * line, line), line)]
        i = lax.rem(d, 16) + 16 * lax.rem(me.core + me.z_lo, 2)
        return remote(src, out.at[:, mine], out_s.at[d], out_r.at[i], (z_lo * 16 + spot, me.z))

    def out_land(d):
        spot = lax.rem(me.yx + lax.rem(d, 16), 16)
        core = lax.rem(me.core + lax.div(d, 16), 2)
        dst = out.at[:, pl.ds(aligned(core * 256 + spot * line, line), line)]
        return remote(dst, dst, out_s.at[d], out_r.at[d], source(d))

    own = pltpu.make_async_copy(
        ship.at[:, me.z_lo, pl.ds(aligned(me.yx * line, line), line)], out.at[:, mine], own_sem.at[0]
    )

    @pl.loop(1, 32)
    def _(d):
        out_copy(d).start()

    @pl.when(stays)
    def _():
        own.start()

    @pl.when(jnp.logical_not(stays))
    def _():
        out_copy(0).start()

    @pl.loop(1, 32)
    def _(d):
        out_land(d).wait_recv()

    @pl.when(stays)
    def _():
        own.wait()

    @pl.when(jnp.logical_not(stays))
    def _():
        out_land(0).wait_recv()
        out_copy(0).wait_send()
        swap_copy().wait_send()

    @pl.loop(1, 32)
    def _(d):
        out_copy(d).wait_send()

    @pl.loop(1, 16)
    def _(d):
        n_copy(d).wait_send()

    @pl.loop(0, 16)
    def _(d):
        for way in (0, 1):
            zn_copy(way, d).wait_send()
            zo_copy(way, d).wait_send()

    for half in (0, 1):
        for d in (1, 2, 3):
            f_copy(half, d).wait_send()
        for df in range(4):
            for way in (0, 1):
                s_copy(half, way, df).wait_send()
                o_copy(half, way, df).wait_send()
            for ds in range(4):
                b_copy(half, df, ds).wait_send()


def in_vmem(count):
    return [pl.BlockSpec(memory_space=pltpu.VMEM)] * count


def per_device(row_queries, row_keys, row_values, residual_in, out_weight, norm_gain, qkv_weight):
    positions, features = row_queries.shape
    share, width = residual_in.shape
    depth = out_weight.shape[0]
    dma = pltpu.SemaphoreType.DMA
    residual_out, normed = pl.pallas_call(
        front,
        out_shape=(
            jax.ShapeDtypeStruct((share, width), BF16),
            jax.ShapeDtypeStruct((share, width), BF16),
        ),
        in_specs=in_vmem(6),
        out_specs=tuple(in_vmem(2)),
        scratch_shapes=[
            pltpu.VMEM((2, COLS, features), BF16),
            pltpu.VMEM((2, COLS, features), BF16),
            pltpu.VMEM((COLS, features), BF16),
            pltpu.VMEM((2 * depth, width), BF16),
            pltpu.VMEM((share, width), F32),
            pltpu.VMEM((share, width), F32),
            pltpu.VMEM((share, width), F32),
            dma((2,)), dma((2,)),
            dma((1,)), dma((1,)),
            dma((3,)), dma((3,)),
            dma((2, 4, 3)), dma((2, 4, 3)),
            dma((2, 2, 16)), dma((2, 2, 16)),
            dma((2, 2, 16)), dma((2, 2, 16)),
            dma((8,)), dma((8,)),
        ],
        compiler_params=pltpu.CompilerParams(
            collective_id=0, has_side_effects=True, vmem_limit_bytes=56 * 2**20
        ),
        name="front",
    )(row_queries, row_keys, row_values, residual_in, out_weight, norm_gain.reshape(1, -1))
    flat = qkv_weight.reshape(qkv_weight.shape[0], -1)
    columns = flat.shape[1]
    column_out = pl.pallas_call(
        back,
        out_shape=jax.ShapeDtypeStruct((2, COLS, features), BF16),
        in_specs=in_vmem(2),
        out_specs=in_vmem(1)[0],
        scratch_shapes=[
            pltpu.VMEM((4, 256, width), BF16),
            pltpu.VMEM((width, columns), BF16),
            pltpu.VMEM((16, 64, columns), BF16),
            pltpu.VMEM((16, 64, features), BF16),
            pltpu.VMEM((2, 2, 256, features), BF16),
            dma((1,)), dma((1,)),
            dma((2, 3)), dma((2, 3)),
            dma((2, 2, 4)), dma((2, 2, 4)),
            dma((2, 2, 4)), dma((2, 2, 4)),
            dma((2, 16)), dma((2, 16)),
            dma((16,)), dma((16,)),
            dma((2, 16)), dma((2, 16)),
            dma((2, 16)), dma((2, 16)),
            dma((32,)), dma((32,)),
            dma((1,)),
        ],
        compiler_params=pltpu.CompilerParams(
            collective_id=1, has_side_effects=True, vmem_limit_bytes=56 * 2**20
        ),
        name="back",
    )(normed, flat)
    return residual_out, column_out.reshape(positions, features)


def solution(mesh):
    placed = (
        P("seq", "head"),
        P("seq", "head"),
        P("seq", "head"),
        P(("seq", "head"), None),
        P("head", "seq"),
        P(),
        P("seq", "head", None, None),
    )
    return jax.shard_map(
        per_device,
        mesh=mesh,
        in_specs=placed,
        out_specs=(P(("seq", "head"), None), P("seq", "head")),
        check_vma=False,
    )
```

```python
import functools

import jax
import jax.numpy as jnp
from jax import lax
from jax.experimental import pallas as pl
from jax.experimental.pallas import tpu as pltpu
from jax.sharding import PartitionSpec as P

HD = 128
COLS = 512
GROUPS = 4
MESH = pl.DeviceIdType.MESH
EPS = 1e-05
EXP2_SCALE = HD ** (-0.5) * 1.4426950408889634
BF16 = jnp.bfloat16
F32 = jnp.float32


def aligned(value, by):
    return pl.multiple_of(value, by)


def ring4(value):
    return lax.rem(value + 8, 4)


class Place:
    def __init__(self):
        self.s = lax.axis_index("seq")
        self.h = lax.axis_index("head")
        self.z_lo = lax.div(self.s, 16)
        self.yx = lax.rem(self.s, 16)
        self.y = lax.div(self.yx, 4)
        self.x = lax.rem(self.s, 4)
        self.z_hi = lax.div(self.h, 2)
        self.core = lax.rem(self.h, 2)
        self.z = self.z_hi * 2 + self.z_lo

    def device(self, z, y, x, core):
        return (lax.rem(z, 2) * 16 + y * 4 + x, lax.div(z, 2) * 2 + core)

    def first(self, half, d):
        if half == 0:
            return self.device(self.z, self.y, ring4(self.x + d), self.core)
        return self.device(self.z, ring4(self.y + d), self.x, self.core)

    def second(self, half, d):
        return self.first(1 - half, d)

    def block(self, half, df, ds):
        if half == 0:
            return ring4(self.y - ds), ring4(self.x - df)
        return ring4(self.y - df), ring4(self.x - ds)

    def shifted(self, axis, d):
        z = ring4(self.z + d) if axis == "z" else self.z
        y = ring4(self.y + d) if axis == "y" else self.y
        x = ring4(self.x + d) if axis == "x" else self.x
        return self.device(z, y, x, self.core)

    def sibling(self):
        return (self.s, self.z_hi * 2 + 1 - self.core)

    def at_z(self, d):
        return self.device(ring4(self.z + d), self.y, self.x, self.core)


def remote(src, dst, send, recv, device):
    return pltpu.make_async_remote_copy(
        src_ref=src, dst_ref=dst, send_sem=send, recv_sem=recv, device_id=device, device_id_type=MESH
    )


def greet(barrier, device):
    pl.semaphore_signal(barrier, inc=1, device_id=device, device_id_type=MESH)


def contract_last(a, b):
    return lax.dot_general(a, b, (((1,), (1,)), ((), ())), preferred_element_type=F32)


def dot(a, b):
    return jnp.dot(a, b, preferred_element_type=F32)


def band_head(queries, keys_prev, keys, values_prev, values, has_prev):
    n = queries.shape[0]
    row = lax.broadcasted_iota(jnp.int32, (n, n), 0)
    col = lax.broadcasted_iota(jnp.int32, (n, n), 1)
    here = col <= row
    back = contract_last(queries, keys_prev)
    back = jnp.where(has_prev, back, -jnp.inf)
    scores = jnp.where(here, contract_last(queries, keys), back)
    top = jnp.max(scores, -1, keepdims=True)
    weights = jnp.exp2((scores - top) * EXP2_SCALE)
    total = jnp.sum(weights, -1, keepdims=True)
    own = jnp.where(here, weights, 0.0).astype(BF16)
    prev = jnp.where(here, 0.0, weights).astype(BF16)
    result = dot(own, values) + dot(prev, values_prev)
    return (result / total).astype(BF16)


PARTS = (
    (0, 192, ("z", "x", "y"), 96),
    (192, 128, ("z", "y", "x"), 0),
    (320, 192, ("x", "y", "z"), 96),
)
LINE = 16


def both(
    q_in, k_in, v_in, res_in, wo, gain, wq, res_hbm, out,
    q, k, v, res, res_out, normed, halo, rows, rows_in, w_out, part, part_in,
    n_buf, w, att, ship,
    in_sem, halo_s, halo_r, row_s, row_r, g1_s, g1_r, g2_s, g2_r, g3_s, g3_r, g4_s, g4_r, p_s, p_r,
    e_s, e_r, f_s, f_r, s_s, s_r, o_s, o_r, b_s, b_r,
    n_s, n_r, zn_s, zn_r, zo_s, zo_r, out_s, out_r,
):
    me = Place()
    here = (me.s, me.h)
    share, width = normed.shape
    depth = wo.shape[0]
    line = LINE
    chunk = 512
    chunks = width // chunk
    last = me.s == 31
    stays = me.z_lo == me.core
    moves = jnp.logical_not(stays)
    k_depth = wq.shape[0]
    half_rows, quarter = k_depth // 2, k_depth // 4

    own_block = w_out.at[
        pl.ds(aligned(me.z_hi * depth, 16), depth), pl.ds(aligned(me.s * 128, 128), 128)
    ]
    loads = [
        pltpu.make_async_copy(wo, own_block, in_sem.at[0]),
        pltpu.make_async_copy(k_in, k, in_sem.at[1]),
        pltpu.make_async_copy(q_in, q, in_sem.at[2]),
        pltpu.make_async_copy(v_in, v, in_sem.at[3]),
        pltpu.make_async_copy(res_in, res, in_sem.at[4]),
    ]
    for load in loads:
        load.start()
    own_rows = pltpu.make_async_copy(
        wq, w.at[pl.ds(aligned(me.s * k_depth, 16), k_depth)], in_sem.at[5]
    )

    @pl.when(stays)
    def _():
        own_rows.start()

    barrier = pltpu.get_barrier_semaphore()

    def landed(ref, sem):
        remote(ref, ref, sem, sem, me.sibling()).wait_recv()

    def gone(ref, sem):
        remote(ref, ref, sem, sem, me.sibling()).wait_send()

    def in_plane(d):
        spot = lax.rem(me.yx + d + 32, 16)
        return me.device(me.z, lax.div(spot, 4), lax.rem(spot, 4), me.core)

    swap = (me.core * 16 + me.yx, me.z_hi * 2 + me.z_lo)

    def source(d):
        spot = lax.rem(me.yx + lax.rem(d, 16), 16)
        core = lax.rem(me.core + lax.div(d, 16), 2)
        return me.device(me.h, lax.div(spot, 4), lax.rem(spot, 4), core)

    @pl.when(me.s > 0)
    def _():
        greet(barrier, (me.s - 1, me.h))

    @pl.loop(1, 16)
    def _(d):
        greet(barrier, in_plane(d))

    for d in (1, 2, 3):
        greet(barrier, me.at_z(d))
    greet(barrier, me.sibling())

    @pl.loop(1, 32)
    def _(d):
        greet(barrier, source(d))

    @pl.when(moves)
    def _():
        greet(barrier, swap)
        greet(barrier, source(0))

    moving = lax.rem(me.z_lo + me.core, 2)
    pl.semaphore_wait(barrier, 15 + 3 + 1 + 31 + 2 * moving + 1 - lax.div(me.s, 31))

    def halo_copy(i):
        which, piece = i // 8, i % 8
        return remote(
            (k_in, v_in)[which].at[8 + piece], halo.at[which, piece], halo_s.at[0], halo_r.at[0],
            (lax.rem(me.s + 1, 32), me.h),
        )

    def halo_start(pieces):
        @pl.when(jnp.logical_not(last))
        def _():
            for i in pieces:
                halo_copy(i).start()

    halo_start(range(2))

    @pl.when(me.s == 0)
    def _():
        halo[...] = jnp.zeros_like(halo)

    def spot_of(p, d1, d2, d3, offset, count):
        back_by = dict(zip(PARTS[p][2], (d1, d2, d3)))
        zz, yy, xx = ring4(me.z - back_by["z"]), ring4(me.y - back_by["y"]), ring4(me.x - back_by["x"])
        return w_out.at[
            pl.ds(aligned(lax.div(zz, 2) * depth + PARTS[p][0] + offset, 16), count),
            pl.ds(aligned((lax.rem(zz, 2) * 16 + yy * 4 + xx) * 128, 128), 128),
        ]

    def g1(p, d, landing=False):
        spot = spot_of(p, d if landing else 0, 0, 0, 0, PARTS[p][1])
        return remote(spot, spot, g1_s.at[p], g1_r.at[p, d - 1], me.shifted(PARTS[p][2][0], d))

    def g2(p, d1, d, landing=False):
        d2 = d if landing else (3 if d == 2 else 0)
        spot = spot_of(p, d1, d2, 0, 0, PARTS[p][1])
        to = me.shifted(PARTS[p][2][1], 3 if d == 2 else d)
        return remote(spot, spot, g2_s.at[p], g2_r.at[p, d1, d - 1], to)

    def g3(p, way, d1, d2, landing=False):
        step = 1 - 2 * way
        spot = spot_of(p, d1, d2, step if landing else 0, 0, PARTS[p][1])
        i = d1 * 4 + d2
        return remote(spot, spot, g3_s.at[p], g3_r.at[p, way, i], me.shifted(PARTS[p][2][2], step))

    def g4(p, way, d1, d2, landing=False):
        step = 1 - 2 * way
        plus = PARTS[p][3]
        offset, count = ((0, plus), (plus, PARTS[p][1] - plus))[way]
        spot = spot_of(p, d1, d2, 2 * step if landing else step, offset, count)
        return remote(spot, spot, g4_s.at[p], g4_r.at[p, way], me.shifted(PARTS[p][2][2], step))

    def far_ways(p):
        return (0, 1) if PARTS[p][3] else (1,)

    def send_on(p, d1, d2):
        for way in (0, 1):
            g3(p, way, d1, d2).start()

    loads[0].wait()
    for p in range(3):
        for d in (1, 3, 2):
            g1(p, d).start()
    for p in range(3):
        for d in (1, 3):
            g2(p, 0, d).start()
    for p in range(3):
        send_on(p, 0, 0)
        halo_start(range(2 + p, 3 + p))

    def swap_copy():
        return remote(
            wq, w.at[pl.ds(aligned(me.s * k_depth, 16), k_depth)], e_s.at[0], e_r.at[0], swap
        )

    @pl.when(moves)
    def _():
        swap_copy().start()

    def attend(top, prev_k, prev_v, prev_top, has_prev):
        for g in range(GROUPS):
            cols = slice(g * HD, (g + 1) * HD)

            def head_of(ref, start):
                return ref[start : start + 8, :, cols].reshape(COLS, HD)

            rows[top // 8, :, cols] = band_head(
                head_of(q, top), head_of(prev_k, prev_top), head_of(k, top),
                head_of(prev_v, prev_top), head_of(v, top), has_prev,
            )

    def row_copy():
        return remote(rows.at[1 - me.z_hi], rows_in, row_s.at[0], row_r.at[0], me.at_z(2))

    for load in loads[1:4]:
        load.wait()
    attend(8, k, v, 0, True)

    @pl.when(me.z_hi == 0)
    def _():
        row_copy().start()

    for d1 in range(1, 4):
        for p in range(3):
            g1(p, d1, True).wait_recv()
            for d in (1, 3):
                g2(p, d1, d).start()
            send_on(p, d1, 0)
        halo_start(range(2 + 3 * d1, 5 + 3 * d1))

    halo_start(range(14, 16))

    @pl.loop(0, 4)
    def _(d1):
        for p in range(3):
            g2(p, d1, 3, True).wait_recv()
            g2(p, d1, 2).start()
            send_on(p, d1, 3)
            g2(p, d1, 1, True).wait_recv()
            send_on(p, d1, 1)

    @pl.loop(0, 4)
    def _(d1):
        for p in range(3):
            g2(p, d1, 2, True).wait_recv()
            send_on(p, d1, 2)

    @pl.when(me.s > 0)
    def _():
        landed(halo, halo_r.at[0])

    attend(0, halo.at[0], halo.at[1], 0, me.s > 0)

    @pl.when(me.z_hi == 1)
    def _():
        row_copy().start()

    for d2 in (0, 3, 1, 2):

        @pl.loop(0, 4)
        def _(d1):
            for p in range(3):
                for way in (0, 1):
                    g3(p, way, d1, d2, True).wait_recv()
                    if way in far_ways(p):
                        g4(p, way, d1, d2).start()

    def slot(core, half, df, ds, offset, count):
        yy, xx = me.block(half, df, ds)
        return w.at[pl.ds(aligned((core * 16 + yy * 4 + xx) * k_depth + offset, 16), count)]

    def swap_land():
        spot = slot(me.core, 0, 0, 0, 0, k_depth)
        return remote(spot, spot, e_s.at[0], e_r.at[0], swap)

    def f_copy(half, d, landing=False):
        spot = slot(me.core, half, d if landing else 0, 0, half * half_rows, half_rows)
        return remote(spot, spot, f_s.at[0], f_r.at[half, d - 1], me.first(half, d))

    def s_copy(half, way, df, landing=False):
        step = 1 - 2 * way
        spot = slot(me.core, half, df, step if landing else 0, half * half_rows, half_rows)
        return remote(spot, spot, s_s.at[0], s_r.at[half, way, df], me.second(half, step))

    def o_copy(half, way, df, landing=False):
        step = 1 - 2 * way
        spot = slot(me.core, half, df, 2 * step if landing else step, half * half_rows + way * quarter, quarter)
        return remote(spot, spot, o_s.at[0], o_r.at[half, way, df], me.second(half, step))

    def b_copy(half, df, ds, landing=False):
        core = 1 - me.core if landing else me.core
        spot = slot(core, half, df, ds, half * half_rows, half_rows)
        return remote(spot, spot, b_s.at[0], b_r.at[0], me.sibling())

    @pl.when(stays)
    def _():
        own_rows.wait()

    @pl.when(moves)
    def _():
        swap_land().wait_recv()

    for half in (0, 1):
        for d in (1, 3, 2):
            f_copy(half, d).start()
    for half in (0, 1):
        for way in (0, 1):
            s_copy(half, way, 0).start()
        b_copy(half, 0, 0).start()

    for p in range(3):
        for way in far_ways(p):
            count = (PARTS[p][3], PARTS[p][1] - PARTS[p][3])[way]
            landed(w_out.at[pl.ds(0, count), pl.ds(0, width // 2)], g4_r.at[p, way])

    row_copy().wait_recv()

    def product(of_core, columns):
        mine = pl.ds(aligned(of_core * share, 16), share)
        kept = dot(rows[me.z_hi, mine, :], w_out[pl.ds(aligned(me.z_hi * depth, 16), depth), columns])
        came = dot(rows_in[mine, :], w_out[pl.ds(aligned((1 - me.z_hi) * depth, 16), depth), columns])
        return kept + came

    def p_copy(n):
        columns = pl.ds(aligned(n * chunk, chunk), chunk)
        return remote(part.at[:, columns], part_in.at[:, columns], p_s.at[0], p_r.at[n], me.sibling())

    @pl.loop(0, chunks)
    def _(n):
        columns = pl.ds(aligned(n * chunk, chunk), chunk)
        part[:, columns] = product(1 - me.core, columns)
        p_copy(n).start()

    loads[4].wait()

    def settle(n, total):
        columns = pl.ds(aligned(n * chunk, chunk), chunk)
        own = product(me.core, columns) + res[:, columns].astype(F32)
        p_copy(n).wait_recv()
        value = (own + part_in[:, columns]).astype(BF16)
        res_out[:, columns] = value
        return total + jnp.sum(value.astype(F32), -1, keepdims=True)

    mean = lax.fori_loop(0, chunks, settle, jnp.zeros((share, 1), F32)) / width
    res_copy = pltpu.make_async_copy(res_out, res_hbm, in_sem.at[6])
    res_copy.start()

    def spread_of(n, total):
        columns = pl.ds(aligned(n * chunk, chunk), chunk)
        center = res_out[:, columns].astype(F32) - mean
        return total + jnp.sum(center * center, -1, keepdims=True)

    variance = lax.fori_loop(0, chunks, spread_of, jnp.zeros((share, 1), F32)) / width
    scale = lax.rsqrt(variance + EPS)

    @pl.loop(0, chunks)
    def _(n):
        columns = pl.ds(aligned(n * chunk, chunk), chunk)
        center = res_out[:, columns].astype(F32) - mean
        normed[:, columns] = (center * scale * gain[:, columns]).astype(BF16)

    def n_spot(dz, d):
        rows = pl.ds(aligned(lax.rem(me.yx - d + 32, 16) * line, line), line)
        return n_buf.at[ring4(me.z - dz), rows]

    def n_copy(d, landing=False):
        if landing:
            spot = n_spot(0, d)
            return remote(spot, spot, n_s.at[0], n_r.at[d], in_plane(d))
        src = normed.at[pl.ds(aligned(lax.rem(me.yx + d, 16) * line, line), line)]
        return remote(src, n_spot(0, 0), n_s.at[0], n_r.at[d], in_plane(d))

    def zn_copy(way, d, landing=False):
        step = 1 - 2 * way
        spot = n_spot(step if landing else 0, d)
        return remote(spot, spot, zn_s.at[way], zn_r.at[way, d], me.at_z(step))

    def zo_copy(way, d, landing=False):
        step = 1 - 2 * way
        spot = n_spot(2 * step if landing else step, d).at[:, pl.ds(way * (width // 2), width // 2)]
        return remote(spot, spot, zo_s.at[way], zo_r.at[way], me.at_z(step))

    n_buf[me.z, pl.ds(aligned(me.yx * line, line), line), :] = normed[
        pl.ds(aligned(me.yx * line, line), line), :
    ]
    for way in (0, 1):
        zn_copy(way, 0).start()

    @pl.loop(1, 6)
    def _(d):
        n_copy(d).start()

    @pl.loop(1, 11)
    def _(d):
        n_copy(d, True).wait_recv()
        for way in (0, 1):
            zn_copy(way, d).start()
        n_copy(d + 5).start()

    @pl.loop(11, 16)
    def _(d):
        n_copy(d, True).wait_recv()
        for way in (0, 1):
            zn_copy(way, d).start()

    for df in (1, 3, 2):
        for half in (0, 1):
            f_copy(half, df, True).wait_recv()
            for way in (0, 1):
                s_copy(half, way, df).start()
            b_copy(half, df, 0).start()
    for df in (0, 1, 3, 2):
        for half in (0, 1):
            for way in (0, 1):
                s_copy(half, way, df, True).wait_recv()
                o_copy(half, way, df).start()
                b_copy(half, df, 1 - 2 * way).start()

    @pl.loop(0, 16)
    def _(d):
        for way in (0, 1):
            zn_copy(way, d, True).wait_recv()
            zo_copy(way, d).start()

    for df in (0, 1, 3, 2):
        for half in (0, 1):
            for way in (0, 1):
                o_copy(half, way, df, True).wait_recv()
            b_copy(half, df, 2).start()

    landed(w.at[pl.ds(0, width // 2)], b_r.at[0])

    size = line * 16
    at = lax.broadcasted_iota(jnp.int32, (size, size), 0)
    to = lax.broadcasted_iota(jnp.int32, (size, size), 1)
    turn = (to == (at & 15) * 16 + (at >> 4)).astype(F32).astype(BF16)
    wide = 6 * HD

    def project(dz):
        zz = ring4(me.z - dz)

        @pl.loop(0, 2)
        def _(n):
            value = dot(n_buf[zz], w[:, pl.ds(aligned(n * wide, wide), wide)]).astype(BF16)
            turned = dot(turn, value).astype(BF16)
            for j in range(2):
                for which, ref in enumerate((q, k, v)):
                    piece = turned[:, (3 * j + which) * HD : (3 * j + which + 1) * HD]
                    ref[
                        :, pl.ds(aligned(zz * 16, 16), 16), pl.ds(aligned((2 * n + j) * HD, HD), HD)
                    ] = piece.reshape(16, 16, HD)

    project(0)
    project(1)
    project(3)

    for way in (0, 1):
        landed(n_buf.at[0, :, pl.ds(0, width // 2)], zo_r.at[way])

    project(2)

    grid_row = 2 * (((at >> 4) & 1) * 16 + (at & 15)) + ((at >> 5) & 1)
    grid_row_k = 2 * (((to >> 4) & 1) * 16 + (to & 15)) + ((to >> 5) & 1)
    allowed = ((at >> 6) == (to >> 6)) & (grid_row_k <= grid_row)

    mine = pl.ds(aligned(me.core * 256 + me.yx * line, line), line)

    def head_columns(g):
        return pl.ds(aligned(g * HD, HD), HD)

    def out_copy(g, d):
        spot = lax.rem(me.yx - lax.rem(d, 16) + 16, 16)
        z_lo = lax.rem(me.z_lo + lax.div(d, 16), 2)
        src = ship.at[:, z_lo, pl.ds(aligned(spot * line, line), line), head_columns(g)]
        dst = out.at[:, mine, head_columns(g)]
        return remote(src, dst, out_s.at[g], out_r.at[g], (z_lo * 16 + spot, me.z))

    def own_copy(g):
        src = ship.at[:, me.z_lo, pl.ds(aligned(me.yx * line, line), line), head_columns(g)]
        return pltpu.make_async_copy(src, out.at[:, mine, head_columns(g)], out_r.at[g])

    @pl.loop(0, GROUPS)
    def _(g):
        cols = head_columns(g)
        for block in range(4):
            some = slice(4 * block, 4 * block + 4)
            queries = q[some, :, cols].reshape(size, HD)
            keys = k[some, :, cols].reshape(size, HD)
            values = v[some, :, cols].reshape(size, HD)
            scores = jnp.where(allowed, contract_last(queries, keys), -jnp.inf)
            top = jnp.max(scores, -1, keepdims=True)
            weights = jnp.exp2((scores - top) * EXP2_SCALE)
            total = jnp.sum(weights, -1, keepdims=True)
            result = (dot(weights.astype(BF16), values) / total).astype(BF16)
            att[some] = result.reshape(4, 64, HD)
        for zz in range(4):
            plane = att[:, zz * 16 : (zz + 1) * 16, :].reshape(size, HD)
            ship[zz // 2, zz % 2, :, cols] = dot(turn, plane).astype(BF16)

        @pl.when(stays)
        def _():
            own_copy(g).start()

        @pl.when(moves)
        def _():
            out_copy(g, 0).start()

        @pl.loop(1, 32)
        def _(d):
            out_copy(g, d).start()

    for g in range(GROUPS):
        landed(out.at[:, :, pl.ds(g * HD, HD)], out_r.at[g])

    @pl.when(stays)
    def _():
        for g in range(GROUPS):
            gone(rows.at[0, pl.ds(0, 31 * 16), pl.ds(0, 256)], out_s.at[g])

    @pl.when(moves)
    def _():
        for g in range(GROUPS):
            gone(rows.at[0, :, pl.ds(0, 256)], out_s.at[g])
        swap_copy().wait_send()

    gone(n_buf.at[0, pl.ds(0, 15 * line)], n_s.at[0])
    for way in (0, 1):
        gone(n_buf.at[0], zn_s.at[way])
        gone(n_buf.at[0, :, pl.ds(0, width // 2)], zo_s.at[way])
    gone(w.at[pl.ds(0, 6 * half_rows)], f_s.at[0])
    gone(w.at[pl.ds(0, 16 * half_rows)], s_s.at[0])
    gone(w.at[pl.ds(0, 16 * quarter)], o_s.at[0])
    gone(w.at[pl.ds(0, 32 * half_rows)], b_s.at[0])
    res_copy.wait()

    @pl.when(jnp.logical_not(last))
    def _():
        gone(halo, halo_s.at[0])

    row_copy().wait_send()
    for p in range(3):
        some = pl.ds(0, PARTS[p][1])
        gone(w_out.at[some, pl.ds(0, 3 * 128)], g1_s.at[p])
        gone(w_out.at[some, pl.ds(0, 12 * 128)], g2_s.at[p])
        gone(w_out.at[some], g3_s.at[p])
        gone(w_out.at[some, pl.ds(0, 16 * 128)], g4_s.at[p])
    gone(part, p_s.at[0])


def per_device(row_queries, row_keys, row_values, residual_in, out_weight, norm_gain, qkv_weight):
    positions, features = row_queries.shape
    share, width = residual_in.shape
    depth = out_weight.shape[0]
    flat = qkv_weight.reshape(qkv_weight.shape[0], -1)
    columns = flat.shape[1]
    dma = pltpu.SemaphoreType.DMA
    anywhere = pl.BlockSpec(memory_space=pl.ANY)
    inside = pl.BlockSpec(memory_space=pltpu.VMEM)

    def folded(array):
        return array.reshape(16, 64, features)

    def pair(sent, received):
        received = received if isinstance(received, tuple) else (received,)
        return [dma((sent,)), dma(received)]

    residual_out, column_out = pl.pallas_call(
        both,
        out_shape=(
            jax.ShapeDtypeStruct((share, width), BF16),
            jax.ShapeDtypeStruct((2, COLS, features), BF16),
        ),
        in_specs=[anywhere] * 5 + [inside, anywhere],
        out_specs=(anywhere, anywhere),
        scratch_shapes=[
            pltpu.VMEM((16, 64, features), BF16),
            pltpu.VMEM((16, 64, features), BF16),
            pltpu.VMEM((16, 64, features), BF16),
            pltpu.VMEM((share, width), BF16),
            pltpu.VMEM((share, width), BF16),
            pltpu.VMEM((share, width), BF16),
            pltpu.VMEM((2, 8, 64, features), BF16),
            pltpu.VMEM((2, COLS, features), BF16),
            pltpu.VMEM((COLS, features), BF16),
            pltpu.VMEM((2 * depth, width), BF16),
            pltpu.VMEM((share, width), F32),
            pltpu.VMEM((share, width), F32),
            pltpu.VMEM((4, 256, width), BF16),
            pltpu.VMEM((width, columns), BF16),
            pltpu.VMEM((16, 64, HD), BF16),
            pltpu.VMEM((2, 2, 256, features), BF16),
            dma((7,)),
            *pair(1, 1), *pair(1, 1),
            *pair(3, (3, 3)), *pair(3, (3, 4, 3)), *pair(3, (3, 2, 16)), *pair(3, (3, 2)), *pair(1, 8),
            *pair(1, 1), *pair(1, (2, 3)), *pair(1, (2, 2, 4)), *pair(1, (2, 2, 4)), *pair(1, 1),
            *pair(1, 16), *pair(2, (2, 16)), *pair(2, 2), *pair(GROUPS, GROUPS),
        ],
        compiler_params=pltpu.CompilerParams(
            collective_id=0, has_side_effects=True, vmem_limit_bytes=60 * 2**20
        ),
        name="both",
    )(
        folded(row_queries), folded(row_keys), folded(row_values),
        residual_in, out_weight, norm_gain.reshape(1, -1), flat,
    )
    return residual_out, column_out.reshape(positions, features)


def solution(mesh):
    placed = (
        P("seq", "head"),
        P("seq", "head"),
        P("seq", "head"),
        P(("seq", "head"), None),
        P("head", "seq"),
        P(),
        P("seq", "head", None, None),
    )
    return jax.shard_map(
        per_device,
        mesh=mesh,
        in_specs=placed,
        out_specs=(P(("seq", "head"), None), P("seq", "head")),
        check_vma=False,
    )
```

```python
import functools

import jax
import jax.numpy as jnp
from jax import lax
from jax.experimental import pallas as pl
from jax.experimental.pallas import tpu as pltpu
from jax.sharding import PartitionSpec as P

HD = 128
COLS = 512
GROUPS = 4
MESH = pl.DeviceIdType.MESH
EPS = 1e-05
EXP2_SCALE = HD ** (-0.5) * 1.4426950408889634
BF16 = jnp.bfloat16
F32 = jnp.float32


def aligned(value, by):
    return pl.multiple_of(value, by)


def ring4(value):
    return lax.rem(value + 8, 4)


class Place:
    def __init__(self):
        self.s = lax.axis_index("seq")
        self.h = lax.axis_index("head")
        self.z_lo = lax.div(self.s, 16)
        self.yx = lax.rem(self.s, 16)
        self.y = lax.div(self.yx, 4)
        self.x = lax.rem(self.s, 4)
        self.z_hi = lax.div(self.h, 2)
        self.core = lax.rem(self.h, 2)
        self.z = self.z_hi * 2 + self.z_lo

    def device(self, z, y, x, core):
        return (lax.rem(z, 2) * 16 + y * 4 + x, lax.div(z, 2) * 2 + core)

    def first(self, half, d):
        if half == 0:
            return self.device(self.z, self.y, ring4(self.x + d), self.core)
        return self.device(self.z, ring4(self.y + d), self.x, self.core)

    def second(self, half, d):
        return self.first(1 - half, d)

    def block(self, half, df, ds):
        if half == 0:
            return ring4(self.y - ds), ring4(self.x - df)
        return ring4(self.y - df), ring4(self.x - ds)

    def shifted(self, axis, d):
        z = ring4(self.z + d) if axis == "z" else self.z
        y = ring4(self.y + d) if axis == "y" else self.y
        x = ring4(self.x + d) if axis == "x" else self.x
        return self.device(z, y, x, self.core)

    def sibling(self):
        return (self.s, self.z_hi * 2 + 1 - self.core)

    def at_z(self, d):
        return self.device(ring4(self.z + d), self.y, self.x, self.core)


def remote(src, dst, send, recv, device):
    return pltpu.make_async_remote_copy(
        src_ref=src, dst_ref=dst, send_sem=send, recv_sem=recv, device_id=device, device_id_type=MESH
    )


def greet(barrier, device):
    pl.semaphore_signal(barrier, inc=1, device_id=device, device_id_type=MESH)


def contract_last(a, b):
    return lax.dot_general(a, b, (((1,), (1,)), ((), ())), preferred_element_type=F32)


def dot(a, b):
    return jnp.dot(a, b, preferred_element_type=F32)


def band_head(queries, keys_prev, keys, values_prev, values, has_prev):
    n = queries.shape[0]
    row = lax.broadcasted_iota(jnp.int32, (n, n), 0)
    col = lax.broadcasted_iota(jnp.int32, (n, n), 1)
    here = col <= row
    back = contract_last(queries, keys_prev)
    back = jnp.where(has_prev, back, -jnp.inf)
    scores = jnp.where(here, contract_last(queries, keys), back)
    top = jnp.max(scores, -1, keepdims=True)
    weights = jnp.exp2((scores - top) * EXP2_SCALE)
    total = jnp.sum(weights, -1, keepdims=True)
    own = jnp.where(here, weights, 0.0).astype(BF16)
    prev = jnp.where(here, 0.0, weights).astype(BF16)
    result = dot(own, values) + dot(prev, values_prev)
    return (result / total).astype(BF16)


PARTS = (
    (0, 224, ("z", "x", "y"), 112),
    (224, 160, ("z", "y", "x"), 0),
    (384, 128, ("x", "y", "z"), 64),
)
LINE = 16


def both(
    q_in, k_in, v_in, res_in, wo, gain, wq, res_hbm, out,
    q, k, v, res, res_out, normed, halo, rows, rows_in, w_out, part, part_in,
    n_buf, w, att, ship, means, scales,
    in_sem, halo_s, halo_r, row_s, row_r, g1_s, g1_r, g2_s, g2_r, g3_s, g3_r, g4_s, g4_r, p_s, p_r,
    e_s, e_r, f_s, f_r, s_s, s_r, o_s, o_r, b_s, b_r,
    n_s, n_r, zn_s, zn_r, zo_s, zo_r, out_s, out_r,
):
    me = Place()
    here = (me.s, me.h)
    share, width = normed.shape
    depth = wo.shape[0]
    line = LINE
    chunk = 512
    chunks = width // chunk
    last = me.s == 31
    stays = me.z_lo == me.core
    moves = jnp.logical_not(stays)
    k_depth = wq.shape[0]
    half_rows, quarter = k_depth // 2, k_depth // 4

    own_block = w_out.at[
        pl.ds(aligned(me.z_hi * depth, 16), depth), pl.ds(aligned(me.s * 128, 128), 128)
    ]
    loads = [
        pltpu.make_async_copy(wo, own_block, in_sem.at[0]),
        pltpu.make_async_copy(k_in, k, in_sem.at[1]),
        pltpu.make_async_copy(q_in, q, in_sem.at[2]),
        pltpu.make_async_copy(v_in, v, in_sem.at[3]),
        pltpu.make_async_copy(res_in, res, in_sem.at[4]),
    ]
    for load in loads:
        load.start()
    own_rows = pltpu.make_async_copy(
        wq, w.at[pl.ds(aligned(me.s * k_depth, 16), k_depth)], in_sem.at[5]
    )

    @pl.when(stays)
    def _():
        own_rows.start()

    barrier = pltpu.get_barrier_semaphore()

    def landed(ref, sem):
        remote(ref, ref, sem, sem, me.sibling()).wait_recv()

    def gone(ref, sem):
        remote(ref, ref, sem, sem, me.sibling()).wait_send()

    def in_plane(d):
        spot = lax.rem(me.yx + d + 32, 16)
        return me.device(me.z, lax.div(spot, 4), lax.rem(spot, 4), me.core)

    swap = (me.core * 16 + me.yx, me.z_hi * 2 + me.z_lo)

    def source(d):
        spot = lax.rem(me.yx + lax.rem(d, 16), 16)
        core = lax.rem(me.core + lax.div(d, 16), 2)
        return me.device(me.h, lax.div(spot, 4), lax.rem(spot, 4), core)

    @pl.when(me.s > 0)
    def _():
        greet(barrier, (me.s - 1, me.h))

    @pl.loop(1, 16)
    def _(d):
        greet(barrier, in_plane(d))

    for d in (1, 2, 3):
        greet(barrier, me.at_z(d))
    greet(barrier, me.sibling())

    @pl.loop(1, 32)
    def _(d):
        greet(barrier, source(d))

    @pl.when(moves)
    def _():
        greet(barrier, swap)
        greet(barrier, source(0))

    moving = lax.rem(me.z_lo + me.core, 2)
    pl.semaphore_wait(barrier, 15 + 3 + 1 + 31 + 2 * moving + 1 - lax.div(me.s, 31))

    def head_slice(g):
        return pl.ds(g * HD, HD)

    def halo_copy(i):
        which, cols = i % 2, head_slice(i // 2)
        return remote(
            (k_in, v_in)[which].at[pl.ds(8, 8), :, cols], halo.at[which, :, :, cols],
            halo_s.at[0], halo_r.at[i], (lax.rem(me.s + 1, 32), me.h),
        )

    def halo_start(pieces):
        @pl.when(jnp.logical_not(last))
        def _():
            for i in pieces:
                halo_copy(i).start()

    halo_start(range(2))

    @pl.when(me.s == 0)
    def _():
        halo[...] = jnp.zeros_like(halo)

    def spot_of(p, d1, d2, d3, offset, count):
        back_by = dict(zip(PARTS[p][2], (d1, d2, d3)))
        zz, yy, xx = ring4(me.z - back_by["z"]), ring4(me.y - back_by["y"]), ring4(me.x - back_by["x"])
        return w_out.at[
            pl.ds(aligned(lax.div(zz, 2) * depth + PARTS[p][0] + offset, 16), count),
            pl.ds(aligned((lax.rem(zz, 2) * 16 + yy * 4 + xx) * 128, 128), 128),
        ]

    def g1(p, d, landing=False):
        spot = spot_of(p, d if landing else 0, 0, 0, 0, PARTS[p][1])
        return remote(spot, spot, g1_s.at[p], g1_r.at[p, d - 1], me.shifted(PARTS[p][2][0], d))

    def g2(p, d1, d, landing=False):
        d2 = d if landing else (3 if d == 2 else 0)
        spot = spot_of(p, d1, d2, 0, 0, PARTS[p][1])
        to = me.shifted(PARTS[p][2][1], 3 if d == 2 else d)
        return remote(spot, spot, g2_s.at[p], g2_r.at[p, d1, d - 1], to)

    def g3(p, way, d1, d2, landing=False):
        step = 1 - 2 * way
        spot = spot_of(p, d1, d2, step if landing else 0, 0, PARTS[p][1])
        i = d1 * 4 + d2
        return remote(spot, spot, g3_s.at[p], g3_r.at[p, way, i], me.shifted(PARTS[p][2][2], step))

    def g4(p, way, d1, d2, landing=False):
        step = 1 - 2 * way
        plus = PARTS[p][3]
        offset, count = ((0, plus), (plus, PARTS[p][1] - plus))[way]
        spot = spot_of(p, d1, d2, 2 * step if landing else step, offset, count)
        return remote(spot, spot, g4_s.at[p], g4_r.at[p, way], me.shifted(PARTS[p][2][2], step))

    def far_ways(p):
        return (0, 1) if PARTS[p][3] else (1,)

    def send_on(p, d1, d2):
        for way in (0, 1):
            g3(p, way, d1, d2).start()

    loads[0].wait()
    for p in range(3):
        for d in (1, 3, 2):
            g1(p, d).start()
    for p in range(3):
        for d in (1, 3):
            g2(p, 0, d).start()
    for p in range(3):
        send_on(p, 0, 0)
        halo_start((2 + p,))

    def swap_copy():
        return remote(
            wq, w.at[pl.ds(aligned(me.s * k_depth, 16), k_depth)], e_s.at[0], e_r.at[0], swap
        )

    @pl.when(moves)
    def _():
        swap_copy().start()

    def attend(top, prev_k, prev_v, has_prev, g):
        cols = slice(g * HD, (g + 1) * HD)

        def head_of(ref, start):
            return ref[start : start + 8, :, cols].reshape(COLS, HD)

        rows[top // 8, :, cols] = band_head(
            head_of(q, top), head_of(prev_k, 0), head_of(k, top), head_of(prev_v, 0), head_of(v, top), has_prev
        )

    def row_copy(g):
        cols = head_slice(g)
        return remote(
            rows.at[1 - me.z_hi, :, cols], rows_in.at[:, cols], row_s.at[0], row_r.at[0], me.at_z(2)
        )

    def second_row(g):
        attend(8, k, v, True, g)

        @pl.when(me.z_hi == 0)
        def _():
            row_copy(g).start()

    def first_row(g):
        @pl.when(me.s > 0)
        def _():
            for i in (2 * g, 2 * g + 1):
                halo_copy(i).wait_recv()

        attend(0, halo.at[0], halo.at[1], me.s > 0, g)

        @pl.when(me.z_hi == 1)
        def _():
            row_copy(g).start()

    for load in loads[1:4]:
        load.wait()
    second_row(0)
    second_row(1)
    for d1 in range(1, 4):
        for p in range(3):
            g1(p, d1, True).wait_recv()
            for d in (1, 3):
                g2(p, d1, d).start()
            send_on(p, d1, 0)
        halo_start((4 + d1,))
    second_row(2)

    @pl.loop(0, 4)
    def _(d1):
        for p in range(3):
            g2(p, d1, 3, True).wait_recv()
            g2(p, d1, 2).start()
            send_on(p, d1, 3)
            g2(p, d1, 1, True).wait_recv()
            send_on(p, d1, 1)

    second_row(3)

    @pl.loop(0, 4)
    def _(d1):
        for p in range(3):
            g2(p, d1, 2, True).wait_recv()
            send_on(p, d1, 2)

    for turn_at, d2 in enumerate((0, 3, 1, 2)):
        first_row(turn_at)

        @pl.loop(0, 4)
        def _(d1):
            for p in range(3):
                for way in (0, 1):
                    g3(p, way, d1, d2, True).wait_recv()
                    if way in far_ways(p):
                        g4(p, way, d1, d2).start()

    def slot(core, half, df, ds, offset, count):
        yy, xx = me.block(half, df, ds)
        return w.at[pl.ds(aligned((core * 16 + yy * 4 + xx) * k_depth + offset, 16), count)]

    def swap_land():
        spot = slot(me.core, 0, 0, 0, 0, k_depth)
        return remote(spot, spot, e_s.at[0], e_r.at[0], swap)

    def f_copy(half, d, landing=False):
        spot = slot(me.core, half, d if landing else 0, 0, half * half_rows, half_rows)
        return remote(spot, spot, f_s.at[0], f_r.at[half, d - 1], me.first(half, d))

    def s_copy(half, way, df, landing=False):
        step = 1 - 2 * way
        spot = slot(me.core, half, df, step if landing else 0, half * half_rows, half_rows)
        return remote(spot, spot, s_s.at[0], s_r.at[half, way, df], me.second(half, step))

    def o_copy(half, way, df, landing=False):
        step = 1 - 2 * way
        spot = slot(me.core, half, df, 2 * step if landing else step, half * half_rows + way * quarter, quarter)
        return remote(spot, spot, o_s.at[0], o_r.at[half, way, df], me.second(half, step))

    def b_copy(half, df, ds, landing=False):
        core = 1 - me.core if landing else me.core
        spot = slot(core, half, df, ds, half * half_rows, half_rows)
        return remote(spot, spot, b_s.at[0], b_r.at[0], me.sibling())

    @pl.when(stays)
    def _():
        own_rows.wait()

    @pl.when(moves)
    def _():
        swap_land().wait_recv()

    for half in (0, 1):
        for d in (1, 3, 2):
            f_copy(half, d).start()
    for half in (0, 1):
        for way in (0, 1):
            s_copy(half, way, 0).start()
        b_copy(half, 0, 0).start()

    for p in range(3):
        for way in far_ways(p):
            count = (PARTS[p][3], PARTS[p][1] - PARTS[p][3])[way]
            landed(w_out.at[pl.ds(0, count), pl.ds(0, width // 2)], g4_r.at[p, way])

    landed(rows_in, row_r.at[0])

    def product(of_core, columns):
        mine = pl.ds(aligned(of_core * share, 16), share)
        kept = dot(rows[me.z_hi, mine, :], w_out[pl.ds(aligned(me.z_hi * depth, 16), depth), columns])
        came = dot(rows_in[mine, :], w_out[pl.ds(aligned((1 - me.z_hi) * depth, 16), depth), columns])
        return kept + came

    def p_copy(n):
        columns = pl.ds(aligned(n * chunk, chunk), chunk)
        return remote(part.at[:, columns], part_in.at[:, columns], p_s.at[0], p_r.at[n], me.sibling())

    @pl.loop(0, chunks)
    def _(n):
        columns = pl.ds(aligned(n * chunk, chunk), chunk)
        part[:, columns] = product(1 - me.core, columns)
        p_copy(n).start()

    loads[4].wait()

    def settle(n, total):
        columns = pl.ds(aligned(n * chunk, chunk), chunk)
        own = product(me.core, columns) + res[:, columns].astype(F32)
        p_copy(n).wait_recv()
        value = (own + part_in[:, columns]).astype(BF16)
        res_out[:, columns] = value
        return total + jnp.sum(value.astype(F32), -1, keepdims=True)

    mean = lax.fori_loop(0, chunks, settle, jnp.zeros((share, 1), F32)) / width
    res_copy = pltpu.make_async_copy(res_out, res_hbm, in_sem.at[6])
    res_copy.start()

    def spread_of(n, total):
        columns = pl.ds(aligned(n * chunk, chunk), chunk)
        center = res_out[:, columns].astype(F32) - mean
        return total + jnp.sum(center * center, -1, keepdims=True)

    variance = lax.fori_loop(0, chunks, spread_of, jnp.zeros((share, 1), F32)) / width
    means[...] = jnp.broadcast_to(mean, means.shape)
    scales[...] = jnp.broadcast_to(lax.rsqrt(variance + EPS), scales.shape)

    def normalize(d):
        block = pl.ds(aligned(lax.rem(me.yx + d, 16) * line, line), line)
        center = res_out[block, :].astype(F32) - means[block, 0:1]
        normed[block, :] = (center * scales[block, 0:1] * gain[...]).astype(BF16)

    def n_spot(dz, d):
        rows = pl.ds(aligned(lax.rem(me.yx - d + 32, 16) * line, line), line)
        return n_buf.at[ring4(me.z - dz), rows]

    def n_copy(d, landing=False):
        if landing:
            spot = n_spot(0, d)
            return remote(spot, spot, n_s.at[0], n_r.at[d], in_plane(d))
        src = normed.at[pl.ds(aligned(lax.rem(me.yx + d, 16) * line, line), line)]
        return remote(src, n_spot(0, 0), n_s.at[0], n_r.at[d], in_plane(d))

    def zn_copy(way, d, landing=False):
        step = 1 - 2 * way
        spot = n_spot(step if landing else 0, d)
        return remote(spot, spot, zn_s.at[way], zn_r.at[way, d], me.at_z(step))

    def zo_copy(way, d, landing=False):
        step = 1 - 2 * way
        spot = n_spot(2 * step if landing else step, d).at[:, pl.ds(way * (width // 2), width // 2)]
        return remote(spot, spot, zo_s.at[way], zo_r.at[way], me.at_z(step))

    normalize(0)
    n_buf[me.z, pl.ds(aligned(me.yx * line, line), line), :] = normed[
        pl.ds(aligned(me.yx * line, line), line), :
    ]
    for way in (0, 1):
        zn_copy(way, 0).start()

    @pl.loop(1, 10)
    def _(d):
        normalize(d)
        n_copy(d).start()

    @pl.loop(10, 16)
    def _(d):
        normalize(d)

    @pl.loop(1, 7)
    def _(d):
        n_copy(d, True).wait_recv()
        for way in (0, 1):
            zn_copy(way, d).start()
        n_copy(d + 9).start()

    @pl.loop(7, 16)
    def _(d):
        n_copy(d, True).wait_recv()
        for way in (0, 1):
            zn_copy(way, d).start()

    for df in (1, 3, 2):
        for half in (0, 1):
            f_copy(half, df, True).wait_recv()
            for way in (0, 1):
                s_copy(half, way, df).start()
            b_copy(half, df, 0).start()
    for df in (0, 1, 3, 2):
        for half in (0, 1):
            for way in (0, 1):
                s_copy(half, way, df, True).wait_recv()
                o_copy(half, way, df).start()
                b_copy(half, df, 1 - 2 * way).start()

    @pl.loop(0, 16)
    def _(d):
        for way in (0, 1):
            zn_copy(way, d, True).wait_recv()
            zo_copy(way, d).start()

    for df in (0, 1, 3, 2):
        for half in (0, 1):
            for way in (0, 1):
                o_copy(half, way, df, True).wait_recv()
            b_copy(half, df, 2).start()

    landed(w.at[pl.ds(0, width // 2)], b_r.at[0])

    size = line * 16
    at = lax.broadcasted_iota(jnp.int32, (size, size), 0)
    to = lax.broadcasted_iota(jnp.int32, (size, size), 1)
    turn = (to == (at & 15) * 16 + (at >> 4)).astype(F32).astype(BF16)
    wide = 6 * HD

    def project_pair(dz, n):
        zz = ring4(me.z - dz)
        value = dot(n_buf[zz], w[:, pl.ds(aligned(n * wide, wide), wide)]).astype(BF16)
        turned = dot(turn, value).astype(BF16)
        for j in range(2):
            for which, ref in enumerate((q, k, v)):
                piece = turned[:, (3 * j + which) * HD : (3 * j + which + 1) * HD]
                ref[
                    :, pl.ds(aligned(zz * 16, 16), 16), pl.ds(aligned((2 * n + j) * HD, HD), HD)
                ] = piece.reshape(16, 16, HD)

    def project(dz):
        @pl.loop(0, 2)
        def _(n):
            project_pair(dz, n)

    project(0)
    project(1)
    project(3)

    for way in (0, 1):
        landed(n_buf.at[0, :, pl.ds(0, width // 2)], zo_r.at[way])

    grid_row = 2 * (((at >> 4) & 1) * 16 + (at & 15)) + ((at >> 5) & 1)
    grid_row_k = 2 * (((to >> 4) & 1) * 16 + (to & 15)) + ((to >> 5) & 1)
    allowed = ((at >> 6) == (to >> 6)) & (grid_row_k <= grid_row)

    mine = pl.ds(aligned(me.core * 256 + me.yx * line, line), line)

    def head_columns(g):
        return pl.ds(aligned(g * HD, HD), HD)

    def out_copy(g, d):
        spot = lax.rem(me.yx - lax.rem(d, 16) + 16, 16)
        z_lo = lax.rem(me.z_lo + lax.div(d, 16), 2)
        src = ship.at[:, z_lo, pl.ds(aligned(spot * line, line), line), head_columns(g)]
        dst = out.at[:, mine, head_columns(g)]
        return remote(src, dst, out_s.at[g], out_r.at[g], (z_lo * 16 + spot, me.z))

    def own_copy(g):
        src = ship.at[:, me.z_lo, pl.ds(aligned(me.yx * line, line), line), head_columns(g)]
        return pltpu.make_async_copy(src, out.at[:, mine, head_columns(g)], out_r.at[g])

    @pl.loop(0, GROUPS)
    def _(g):
        @pl.when(lax.rem(g, 2) == 0)
        def _():
            project_pair(2, lax.div(g, 2))

        cols = head_columns(g)
        for block in range(4):
            some = slice(4 * block, 4 * block + 4)
            queries = q[some, :, cols].reshape(size, HD)
            keys = k[some, :, cols].reshape(size, HD)
            values = v[some, :, cols].reshape(size, HD)
            scores = jnp.where(allowed, contract_last(queries, keys), -jnp.inf)
            top = jnp.max(scores, -1, keepdims=True)
            weights = jnp.exp2((scores - top) * EXP2_SCALE)
            total = jnp.sum(weights, -1, keepdims=True)
            result = (dot(weights.astype(BF16), values) / total).astype(BF16)
            att[some] = result.reshape(4, 64, HD)
        for zz in range(4):
            plane = att[:, zz * 16 : (zz + 1) * 16, :].reshape(size, HD)
            ship[zz // 2, zz % 2, :, cols] = dot(turn, plane).astype(BF16)

        @pl.when(stays)
        def _():
            own_copy(g).start()

        @pl.when(moves)
        def _():
            out_copy(g, 0).start()

        @pl.loop(1, 32)
        def _(d):
            out_copy(g, d).start()

    for g in range(GROUPS):
        landed(out.at[:, :, pl.ds(g * HD, HD)], out_r.at[g])

    @pl.when(stays)
    def _():
        for g in range(GROUPS):
            gone(rows.at[0, pl.ds(0, 31 * 16), pl.ds(0, 256)], out_s.at[g])

    @pl.when(moves)
    def _():
        for g in range(GROUPS):
            gone(rows.at[0, :, pl.ds(0, 256)], out_s.at[g])
        swap_copy().wait_send()

    gone(n_buf.at[0, pl.ds(0, 15 * line)], n_s.at[0])
    for way in (0, 1):
        gone(n_buf.at[0], zn_s.at[way])
        gone(n_buf.at[0, :, pl.ds(0, width // 2)], zo_s.at[way])
    gone(w.at[pl.ds(0, 6 * half_rows)], f_s.at[0])
    gone(w.at[pl.ds(0, 16 * half_rows)], s_s.at[0])
    gone(w.at[pl.ds(0, 16 * quarter)], o_s.at[0])
    gone(w.at[pl.ds(0, 32 * half_rows)], b_s.at[0])
    res_copy.wait()

    @pl.when(jnp.logical_not(last))
    def _():
        gone(halo, halo_s.at[0])

    gone(rows_in, row_s.at[0])
    for p in range(3):
        some = pl.ds(0, PARTS[p][1])
        gone(w_out.at[some, pl.ds(0, 3 * 128)], g1_s.at[p])
        gone(w_out.at[some, pl.ds(0, 12 * 128)], g2_s.at[p])
        gone(w_out.at[some], g3_s.at[p])
        gone(w_out.at[some, pl.ds(0, 16 * 128)], g4_s.at[p])
    gone(part, p_s.at[0])


def per_device(row_queries, row_keys, row_values, residual_in, out_weight, norm_gain, qkv_weight):
    positions, features = row_queries.shape
    share, width = residual_in.shape
    depth = out_weight.shape[0]
    flat = qkv_weight.reshape(qkv_weight.shape[0], -1)
    columns = flat.shape[1]
    dma = pltpu.SemaphoreType.DMA
    anywhere = pl.BlockSpec(memory_space=pl.ANY)
    inside = pl.BlockSpec(memory_space=pltpu.VMEM)

    def folded(array):
        return array.reshape(16, 64, features)

    def pair(sent, received):
        received = received if isinstance(received, tuple) else (received,)
        return [dma((sent,)), dma(received)]

    residual_out, column_out = pl.pallas_call(
        both,
        out_shape=(
            jax.ShapeDtypeStruct((share, width), BF16),
            jax.ShapeDtypeStruct((2, COLS, features), BF16),
        ),
        in_specs=[anywhere] * 5 + [inside, anywhere],
        out_specs=(anywhere, anywhere),
        scratch_shapes=[
            pltpu.VMEM((16, 64, features), BF16),
            pltpu.VMEM((16, 64, features), BF16),
            pltpu.VMEM((16, 64, features), BF16),
            pltpu.VMEM((share, width), BF16),
            pltpu.VMEM((share, width), BF16),
            pltpu.VMEM((share, width), BF16),
            pltpu.VMEM((2, 8, 64, features), BF16),
            pltpu.VMEM((2, COLS, features), BF16),
            pltpu.VMEM((COLS, features), BF16),
            pltpu.VMEM((2 * depth, width), BF16),
            pltpu.VMEM((share, width), F32),
            pltpu.VMEM((share, width), F32),
            pltpu.VMEM((4, 256, width), BF16),
            pltpu.VMEM((width, columns), BF16),
            pltpu.VMEM((16, 64, HD), BF16),
            pltpu.VMEM((2, 2, 256, features), BF16),
            pltpu.VMEM((share, 128), F32),
            pltpu.VMEM((share, 128), F32),
            dma((7,)),
            *pair(1, 8), *pair(1, 1),
            *pair(3, (3, 3)), *pair(3, (3, 4, 3)), *pair(3, (3, 2, 16)), *pair(3, (3, 2)), *pair(1, 8),
            *pair(1, 1), *pair(1, (2, 3)), *pair(1, (2, 2, 4)), *pair(1, (2, 2, 4)), *pair(1, 1),
            *pair(1, 16), *pair(2, (2, 16)), *pair(2, 2), *pair(GROUPS, GROUPS),
        ],
        compiler_params=pltpu.CompilerParams(
            collective_id=0, has_side_effects=True, vmem_limit_bytes=60 * 2**20
        ),
        name="both",
    )(
        folded(row_queries), folded(row_keys), folded(row_values),
        residual_in, out_weight, norm_gain.reshape(1, -1), flat,
    )
    return residual_out, column_out.reshape(positions, features)


def solution(mesh):
    placed = (
        P("seq", "head"),
        P("seq", "head"),
        P("seq", "head"),
        P(("seq", "head"), None),
        P("head", "seq"),
        P(),
        P("seq", "head", None, None),
    )
    return jax.shard_map(
        per_device,
        mesh=mesh,
        in_specs=placed,
        out_specs=(P(("seq", "head"), None), P("seq", "head")),
        check_vma=False,
    )
```
